256 devices in a mesh: blk: 16 (over y_hi, z), rows: 16 (over x, y_lo, core).
Axes of the slice: x: 4, y: 4 (y_hi: 2, y_lo: 2; y = y_hi * 2 + y_lo), z: 8, core: 2. Of those that a mesh axis runs over, the one named last changes fastest.
Arguments:
- operator: float32 [16384, 16384], P('rows', 'blk'), may hold values from -60 to 60
Outputs:
- rotated: float32 [16384, 16384], P('rows', 'blk')
The draws below stay inside these ranges and needn't reach their ends.
All inputs are finite; a program needn't handle non-finite values.
Results may differ from the reference program's by a relative error of at most 0.0001.
Values sent between devices are 32-bit elements; how exact they have to be, the bound alone decides.
A program may use at most 64 MiB of HBM per device.

```python
import math
import jax
import jax.numpy as jnp
from jax import lax

BW = 256
PAIRS_DEV = 2
ROUNDS = 2
NS_STEPS = 1
M = 16384
N_BLK = 16


def draw_operator(key, part):
    key = jax.random.fold_in(key, 11)
    first, second = jax.random.split(key)
    entries = jnp.clip(jax.random.normal(first, (M, M), jnp.float32), -4.0, 4.0)
    scales = jnp.exp(jax.random.uniform(second, (M,), jnp.float32, 0.0, 0.5 * math.log(10.0)))
    symmetric = (entries + entries.T) * 0.70710678
    return symmetric * scales[:, None] * scales[None, :]


def setup_inputs(seed: int = 0) -> dict:
    splits = jax.random.split(jax.random.key(seed), 2)
    operator = draw_operator(jax.random.fold_in(splits[1], 71), 0)
    return {"operator": operator}


HIGH = lax.Precision.HIGHEST

def rotation(coupling, upper_squares, lower_squares):
    width = coupling.shape[0]
    mixing = -coupling / (upper_squares[:, None] + lower_squares[None, :] + 1e-06)
    factor = jnp.sqrt(1.0 + jnp.sum(mixing * mixing))
    eye = jnp.eye(width, dtype=jnp.float32)
    top_row = jnp.concatenate([eye, mixing], axis=1)
    bottom_row = jnp.concatenate([-mixing.T, eye], axis=1)
    ortho = jnp.concatenate([top_row, bottom_row], axis=0) / factor
    for sweep in range(NS_STEPS):
        square = jnp.dot(ortho.T, ortho, precision=HIGH, preferred_element_type=jnp.float32)
        ortho = 1.5 * ortho - 0.5 * jnp.dot(ortho, square, precision=HIGH, preferred_element_type=jnp.float32)
    return ortho

def rotate_pair(blocks):
    upper, lower = blocks
    coupling = jnp.dot(upper.T, lower, precision=HIGH, preferred_element_type=jnp.float32)
    ortho = rotation(coupling, lax.optimization_barrier(jnp.sum(upper * upper, axis=0)), lax.optimization_barrier(jnp.sum(lower * lower, axis=0)))
    paired = jnp.concatenate([upper, lower], axis=1)
    turned = jnp.dot(paired, ortho, precision=HIGH, preferred_element_type=jnp.float32)
    return (turned[:, :BW], turned[:, BW:])

def reference(operator):
    total_slots = PAIRS_DEV * N_BLK
    slots = operator.reshape(M, total_slots, 2, BW).transpose(1, 2, 0, 3)
    uppers = slots[:, 0]
    lowers = slots[:, 1]
    for sweep in range(ROUNDS):
        uppers, lowers = lax.map(rotate_pair, (uppers, lowers))
        if sweep + 1 < ROUNDS:
            new_uppers = jnp.concatenate([uppers[0:1], lowers[0:1], uppers[1:total_slots - 1]], axis=0)
            new_lowers = jnp.concatenate([lowers[1:], uppers[total_slots - 1:total_slots]], axis=0)
            uppers, lowers = (new_uppers, new_lowers)
    stacked = jnp.stack([uppers, lowers], axis=1)
    return stacked.transpose(2, 0, 1, 3).reshape(M, M)
```

```python
import functools

import jax
import jax.numpy as jnp
from jax import lax
from jax.experimental import pallas as pl
from jax.experimental.pallas import tpu as pltpu
from jax.sharding import PartitionSpec as P

BW = 256
HB = 128
MESH = pl.DeviceIdType.MESH
F32 = jnp.float32
BF16 = jnp.bfloat16
FAR = (5, 4, 3, 7, 1, 2, 6)


def dot(a, b, contract):
    return lax.dot_general(a, b, (contract, ((), ())), preferred_element_type=F32)


NN = ((1,), (0,))
NT = ((1,), (1,))
TN = ((0,), (0,))


def split(value):
    high = value.astype(BF16)
    return high, (value - high.astype(F32)).astype(BF16)


def eye(rows, columns):
    return lax.broadcasted_iota(jnp.int32, (rows, columns), 0) == lax.broadcasted_iota(
        jnp.int32, (rows, columns), 1
    )


def write_rotation(x, w_ref):
    xh, xl = split(x)
    total = jnp.sum(jnp.sum(x * x, axis=0, keepdims=True), axis=1, keepdims=True)
    inv = 1.0 / jnp.sqrt(1.0 + total)
    b = 0.5 * inv * inv * inv
    a = 1.5 * inv - b
    left = dot(
        jnp.concatenate([xh, xl, xh], axis=1), jnp.concatenate([xh, xh, xl], axis=1), NT
    )
    right = dot(
        jnp.concatenate([xh, xl, xh], axis=0), jnp.concatenate([xh, xh, xl], axis=0), TN
    )
    lh, ll = split(left)
    cube = dot(
        jnp.concatenate([lh, ll, lh], axis=1), jnp.concatenate([xh, xh, xl], axis=0), NN
    )
    z = a * x - b * cube
    diagonal = jnp.where(eye(BW, BW), jnp.broadcast_to(a, (BW, BW)), 0.0)
    parts = (
        (0, 0, diagonal - b * left),
        (0, BW, z),
        (BW, 0, -z.T),
        (BW, BW, diagonal - b * right),
    )
    for row, column, value in parts:
        high, low = split(value)
        w_ref[row : row + BW, column : column + BW] = high
        w_ref[2 * BW + row : 3 * BW + row, column : column + BW] = low


def turn(hl, w_ref, column):
    wh = w_ref[0 : 2 * BW, column : column + BW]
    wl = w_ref[2 * BW : 4 * BW, column : column + BW]
    return dot(
        jnp.concatenate([hl, hl[:, : 2 * BW]], axis=1),
        jnp.concatenate([wh, wh, wl], axis=0),
        NN,
    )


def gram(ah, al, bh, bl):
    both = dot(ah, jnp.concatenate([bh, bl], axis=1), TN)
    return both[:, :BW] + both[:, BW:] + dot(al, bh, TN)


def pack(ts, slot, t, g, h):
    size = t.shape[0] // 4
    line = lax.broadcasted_iota(jnp.int32, (8, HB), 0)
    for j in range(8):
        half, quarter = j // 4, j % 4
        ts[slot, j, 0:size, :] = t[quarter * size : (quarter + 1) * size, half * HB : (half + 1) * HB]
        start = quarter * size
        wide = jnp.broadcast_to(g[:, start // HB * HB : start // HB * HB + HB], (8, HB))
        if start % HB:
            wide = pltpu.roll(wide, HB - start % HB, 1)
        lower = jnp.broadcast_to(h[:, half * HB : (half + 1) * HB], (8, HB))
        ts[slot, j, size : size + 8, :] = jnp.where(line == 0, wide, lower)


def jacobi(
    op, hl_out, x_out,
    pin, hl1, hl2, w, sb, ra, rl, hsum,
    ts0, ts1, ts2, tr0, tr1, tr2, rs0, rs1, rs2, rd0, rd1, rd2, xb0, xb1, xb2,
    load_sem, out_sem, core_send, core_recv, rs_send, rs_recv, ag_send, ag_recv,
    fw_send, fw_recv, z_send, z_recv, rl_send, rl_recv,
):
    blk = lax.axis_index("blk")
    rows = lax.axis_index("rows")
    blocks = lax.axis_size("blk")
    last = blocks - 1
    middle = blocks // 2
    is_relay = (blk == 0) | (blk == last)
    is_middle = (blk == middle - 1) | (blk == middle)
    core = rows % 2
    chip = rows // 2
    px, py = rows // 4, chip % 2
    sibling = (blk, chip * 2 + 1 - core)
    other = 1 - core
    slots = (other, core)

    def mate(k):
        return ((px + k // 2) % 4) * 2 + (py + k % 2) % 2

    def source(k):
        return ((px + 4 - k // 2) % 4) * 2 + (py + k % 2) % 2

    loads = {}
    for i, slot in enumerate(slots):
        shift = jnp.where((slot == 0) & (blk > 0), BW, 0)
        for part, column in enumerate((slot * 2 * BW + shift, slot * 2 * BW + BW - shift)):
            loads[i, part] = pltpu.make_async_copy(
                op.at[:, pl.ds(pl.multiple_of(column, BW), BW)],
                pin.at[slot, part],
                load_sem.at[slot, part],
            )
            loads[i, part].start()

    barrier = pltpu.get_barrier_semaphore()
    pl.semaphore_signal(barrier, inc=1, device_id=sibling, device_id_type=MESH)
    for k in FAR:
        pl.semaphore_signal(
            barrier, inc=1, device_id=(blk, mate(k) * 2 + core), device_id_type=MESH
        )

    @pl.when(blk > 0)
    def _():
        pl.semaphore_signal(barrier, inc=1, device_id=(blk - 1, rows), device_id_type=MESH)

    @pl.when(blk < last)
    def _():
        pl.semaphore_signal(barrier, inc=1, device_id=(blk + 1, rows), device_id_type=MESH)

    @pl.when(is_relay)
    def _():
        for side in range(2):
            pl.semaphore_signal(
                barrier, inc=1, device_id=(middle - side, rows), device_id_type=MESH
            )

    @pl.when(is_middle)
    def _():
        for end in (0, last):
            pl.semaphore_signal(barrier, inc=1, device_id=(end, rows), device_id_type=MESH)

    greetings = 8 + jnp.where(blk > 0, 1, 0) + jnp.where(blk < last, 1, 0)
    greetings = greetings + jnp.where(is_relay | is_middle, 2, 0)
    pending = []

    def remote(src, dst, send, recv, target):
        return pltpu.make_async_remote_copy(
            src_ref=src, dst_ref=dst, send_sem=send, recv_sem=recv,
            device_id=target, device_id_type=MESH,
        )

    def core_copy(i, ts, tr):
        return remote(ts.at[other], tr, core_send.at[i], core_recv.at[i], sibling)

    def reduce_own(i, ts, tr, rs, rd, xb, sign):
        size = rs.shape[1] - 8
        core_copy(i, ts, tr).wait_recv()
        for k in FAR:
            rs[mate(k)] = ts[core, mate(k)] + tr[mate(k)]
            copy = remote(
                rs.at[mate(k)], rd.at[k], rs_send.at[i, k], rs_recv.at[i, k],
                (blk, mate(k) * 2 + core),
            )
            copy.start()
            pending.append(copy)
        total = ts[core, chip] + tr[chip]
        for k in FAR[::-1]:
            remote(
                rs.at[mate(k)], rd.at[k], rs_send.at[i, k], rs_recv.at[i, k],
                (blk, mate(k) * 2 + core),
            ).wait_recv()
            total = total + rd[k]
        g = jnp.sum(
            jnp.where(eye(size, HB), jnp.broadcast_to(total[size : size + 1], (size, HB)), 0.0),
            axis=1, keepdims=True,
        )
        h = total[size + 1 : size + 2]
        xb[core, chip] = sign * total[:size] / (g + h + 1e-06)
        for k in FAR:
            copy = remote(
                xb.at[core, chip], xb.at[core, chip], ag_send.at[i, k], ag_recv.at[i, k],
                (blk, mate(k) * 2 + core),
            )
            copy.start()
            pending.append(copy)
        copy = remote(
            xb.at[core, chip], xb.at[core, chip], fw_send.at[i, 0], fw_recv.at[i, 0], sibling
        )
        copy.start()
        pending.append(copy)

    def hand_on(i, xb):
        for k in FAR[::-1]:
            piece = xb.at[core, source(k)]
            remote(
                piece, piece, ag_send.at[i, k], ag_recv.at[i, k], (blk, mate(k) * 2 + core)
            ).wait_recv()
            copy = remote(piece, piece, fw_send.at[i, k], fw_recv.at[i, k], sibling)
            copy.start()
            pending.append(copy)

    def receive_other(i, xb):
        for k in (0,) + FAR[::-1]:
            piece = xb.at[other, source(k)]
            remote(piece, piece, fw_send.at[i, k], fw_recv.at[i, k], sibling).wait_recv()

    for i, slot in enumerate(slots):
        loads[i, 0].wait()
        loads[i, 1].wait()

        def part(n, sums, slot=slot):
            at = pl.ds(pl.multiple_of(n * HB, HB), HB)
            out = []
            for p in range(2):
                value = pin[slot, p, at, :]
                high, low = split(value)
                hl1[slot, at, p * BW : (p + 1) * BW] = high
                hl1[slot, at, (2 + p) * BW : (3 + p) * BW] = low
                out.append(sums[p] + jnp.sum(value * value, axis=0, keepdims=True))
            return tuple(out)

        zero = jnp.zeros((1, BW), F32)
        g, h = lax.fori_loop(0, pin.shape[2] // HB, part, (zero, zero))
        t = gram(
            hl1[slot, :, 0:BW], hl1[slot, :, 2 * BW : 3 * BW],
            hl1[slot, :, BW : 2 * BW], hl1[slot, :, 3 * BW : 4 * BW],
        )
        pack(ts0, slot, t, g, h)
        if i == 0:
            pl.semaphore_wait(barrier, greetings)
            copy = core_copy(0, ts0, tr0)
            copy.start()
            pending.append(copy)
    sign = jnp.where((core == 0) & (blk > 0), 1.0, -1.0)
    reduce_own(0, ts0, tr0, rs0, rd0, xb0, sign)
    hand_on(0, xb0)

    half_rows = pin.shape[2] // 2

    def z_away(slot, column, m):
        at = pl.ds(m * half_rows, half_rows)
        return remote(
            sb.at[slot, column, at], ra.at[1 - slot, column, at],
            z_send.at[slot, column, m], z_recv.at[1 - slot, column, m],
            (jnp.clip(blk + 2 * slot - 1, 0, last), rows),
        )

    def z_here(slot, column, m):
        at = pl.ds(m * half_rows, half_rows)
        return pltpu.make_async_copy(
            sb.at[slot, column, at], ra.at[slot, column, at], z_recv.at[slot, column, m]
        )

    def at_edge(slot):
        return blk == slot * last

    def z_start(slot, column, m):
        @pl.when(at_edge(slot))
        def _():
            z_here(slot, column, m).start()

        if m == 0:

            @pl.when(jnp.logical_not(at_edge(slot)))
            def _():
                z_away(slot, column, m).start()

        else:

            @pl.when(jnp.logical_not(at_edge(slot) | (blk == middle - slot)))
            def _():
                z_away(slot, column, m).start()

            @pl.when(blk == middle - slot)
            def _():
                remote(
                    sb.at[slot, column, pl.ds(half_rows, half_rows)], rl.at[column],
                    z_send.at[slot, column, 1], rl_recv.at[column], (last * slot, rows),
                ).start()

    def relay(column):
        goal = jnp.where(blk == last, 0, 1)
        return remote(
            rl.at[column], ra.at[goal, column, pl.ds(half_rows, half_rows)],
            rl_send.at[column], z_recv.at[goal, column, 1], (middle - goal, rows),
        )

    def pass_on(column):
        @pl.when(is_relay)
        def _():
            remote(
                rl.at[column], rl.at[column], rl_send.at[column], rl_recv.at[column], sibling
            ).wait_recv()
            relay(column).start()

    def z_wait_recv(slot, column, m):
        at = pl.ds(m * half_rows, half_rows)

        @pl.when(at_edge(slot))
        def _():
            z_here(slot, column, m).wait()

        @pl.when(jnp.logical_not(at_edge(slot)))
        def _():
            remote(
                sb.at[slot, column, at], ra.at[slot, column, at],
                z_send.at[slot, column, m], z_recv.at[slot, column, m], sibling,
            ).wait_recv()

    for i, slot in enumerate((core, other)):
        if i == 1:
            receive_other(0, xb0)
        x = jnp.concatenate(
            [jnp.concatenate([xb0[slot, 4 * p + n] for n in range(4)], axis=0) for p in range(2)],
            axis=1,
        )
        write_rotation(x, w.at[slot])
        for m in range(2):
            at = pl.ds(m * half_rows, half_rows)
            moved = turn(hl1[slot, at, :], w.at[slot], 0)
            sb[slot, 0, at, :] = moved[:, :HB]
            z_start(slot, 0, m)
            sb[slot, 1, at, :] = moved[:, HB:]
    for slot in (core, other):
        for m in range(2):
            z_start(slot, 1, m)
    for slot in (core, other):
        h = jnp.zeros((1, BW), F32)
        for m in range(2):
            at = pl.ds(m * half_rows, half_rows)
            kept = turn(hl1[slot, at, :], w.at[slot], BW)
            high, low = split(kept)
            hl2[1 - slot, at, BW : 2 * BW] = high
            hl2[1 - slot, at, 3 * BW : 4 * BW] = low
            h = h + jnp.sum(kept * kept, axis=0, keepdims=True)
        hsum[1 - slot] = jnp.broadcast_to(h, (8, BW))

    pass_on(0)
    sign = jnp.where(core == 0, -1.0, 1.0)
    second = ((ts1, tr1, rs1, rd1, xb1), (ts2, tr2, rs2, rd2, xb2))
    for column, (ts, tr, rs, rd, xb) in enumerate(second):
        for i, slot in enumerate(slots):
            for m in range(2):
                z_wait_recv(slot, column, m)

            def part(n, g, slot=slot, column=column):
                at = pl.ds(pl.multiple_of(n * HB, HB), HB)
                value = ra[slot, column, at, :]
                high, low = split(value)
                hl2[slot, at, column * HB : (column + 1) * HB] = high
                hl2[slot, at, 2 * BW + column * HB : 2 * BW + (column + 1) * HB] = low
                return g + jnp.sum(value * value, axis=0, keepdims=True)

            g = lax.fori_loop(0, pin.shape[2] // HB, part, jnp.zeros((1, HB), F32))
            t = gram(
                hl2[slot, :, column * HB : (column + 1) * HB],
                hl2[slot, :, 2 * BW + column * HB : 2 * BW + (column + 1) * HB],
                hl2[slot, :, BW : 2 * BW], hl2[slot, :, 3 * BW : 4 * BW],
            )
            pack(ts, slot, t, g, hsum[slot, 0:1, :])
            if i == 0:
                copy = core_copy(1 + column, ts, tr)
                copy.start()
                pending.append(copy)
        if column == 0:
            pass_on(1)
        if column == 1:
            whole = pltpu.make_async_copy(hl2, hl_out, out_sem.at[0])
            whole.start()
            hand_on(1, xb1)
        reduce_own(1 + column, ts, tr, rs, rd, xb, sign)
    hand_on(2, xb2)
    outs = []
    for column, xb in enumerate((xb1, xb2)):
        receive_other(1 + column, xb)
        copy = pltpu.make_async_copy(xb, x_out.at[column], out_sem.at[1 + column])
        copy.start()
        outs.append(copy)
    for copy in pending:
        copy.wait_send()
    for slot in range(2):
        for column in range(2):
            for m in range(2):

                @pl.when(jnp.logical_not(at_edge(slot)))
                def _():
                    z_away(slot, column, m).wait_send()

    @pl.when(is_relay)
    def _():
        for column in range(2):
            relay(column).wait_send()

    whole.wait()
    for copy in outs:
        copy.wait()


def finish(hl_in, x_in, out, hl, xv, w, ob, hl_sem, x_sem, out_sem):
    count = 2
    size = hl.shape[1] // count
    x_copy = pltpu.make_async_copy(x_in, xv, x_sem)
    x_copy.start()
    loads = {}
    for slot in range(2):
        for m in range(count):
            at = pl.ds(m * size, size)
            loads[slot, m] = pltpu.make_async_copy(
                hl_in.at[slot, at], hl.at[slot, at], hl_sem.at[slot, m]
            )
            loads[slot, m].start()
    x_copy.wait()
    stores = []
    for slot in range(2):
        x = jnp.concatenate(
            [
                jnp.concatenate(
                    [xv[column, slot, 4 * p + n] for column in range(2) for n in range(4)], axis=0
                )
                for p in range(2)
            ],
            axis=1,
        )
        write_rotation(x, w.at[slot])
        for m in range(count):
            at = pl.ds(m * size, size)
            loads[slot, m].wait()
            lhs = hl[slot, at, :]
            first = slot * 2 * BW
            for p in range(2):
                column = first + (p * BW if slot == 0 else BW - p * BW)
                ob[at, column : column + BW] = turn(lhs, w.at[slot], p * BW)
            copy = pltpu.make_async_copy(
                ob.at[at, pl.ds(first, 2 * BW)],
                out.at[at, pl.ds(first, 2 * BW)],
                out_sem.at[slot, m],
            )
            copy.start()
            stores.append(copy)
    for copy in stores:
        copy.wait()


def local(operator):
    rows = operator.shape[0]
    any_spec = pl.BlockSpec(memory_space=pl.ANY)
    dma = pltpu.SemaphoreType.DMA

    def per_step(make):
        return [make(64), make(32), make(32)]

    hl, x = pl.pallas_call(
        jacobi,
        out_shape=(
            jax.ShapeDtypeStruct((2, rows, 4 * BW), BF16),
            jax.ShapeDtypeStruct((2, 2, 8, 32, HB), F32),
        ),
        in_specs=[any_spec],
        out_specs=(any_spec, any_spec),
        scratch_shapes=[
            pltpu.VMEM((2, 2, rows, BW), F32),
            pltpu.VMEM((2, rows, 4 * BW), BF16),
            pltpu.VMEM((2, rows, 4 * BW), BF16),
            pltpu.VMEM((2, 4 * BW, 2 * BW), BF16),
            pltpu.VMEM((2, 2, rows, HB), F32),
            pltpu.VMEM((2, 2, rows, HB), F32),
            pltpu.VMEM((2, rows // 2, HB), F32),
            pltpu.VMEM((2, 8, BW), F32),
            *per_step(lambda size: pltpu.VMEM((2, 8, size + 8, HB), F32)),
            *per_step(lambda size: pltpu.VMEM((8, size + 8, HB), F32)),
            *per_step(lambda size: pltpu.VMEM((8, size + 8, HB), F32)),
            *per_step(lambda size: pltpu.VMEM((8, size + 8, HB), F32)),
            *per_step(lambda size: pltpu.VMEM((2, 8, size, HB), F32)),
            dma((2, 2)),
            dma((3,)),
            dma((3,)),
            dma((3,)),
            dma((3, 8)),
            dma((3, 8)),
            dma((3, 8)),
            dma((3, 8)),
            dma((3, 8)),
            dma((3, 8)),
            dma((2, 2, 2)),
            dma((2, 2, 2)),
            dma((2,)),
            dma((2,)),
        ],
        compiler_params=pltpu.CompilerParams(
            collective_id=0, has_side_effects=True, vmem_limit_bytes=48 * 2**20
        ),
        name="jacobi",
    )(operator)
    return pl.pallas_call(
        finish,
        out_shape=jax.ShapeDtypeStruct(operator.shape, F32),
        in_specs=[any_spec, any_spec],
        out_specs=any_spec,
        scratch_shapes=[
            pltpu.VMEM((2, rows, 4 * BW), BF16),
            pltpu.VMEM((2, 2, 8, 32, HB), F32),
            pltpu.VMEM((2, 4 * BW, 2 * BW), BF16),
            pltpu.VMEM((rows, 4 * BW), F32),
            dma((2, 2)),
            dma,
            dma((2, 2)),
        ],
        compiler_params=pltpu.CompilerParams(vmem_limit_bytes=40 * 2**20),
        name="finish",
    )(hl, x)


def solution(mesh):
    placed = P("rows", "blk")
    return jax.shard_map(local, mesh=mesh, in_specs=(placed,), out_specs=placed, check_vma=False)
```

```python
import functools

import jax
import jax.numpy as jnp
from jax import lax
from jax.experimental import pallas as pl
from jax.experimental.pallas import tpu as pltpu
from jax.sharding import PartitionSpec as P

BW = 256
HB = 128
MESH = pl.DeviceIdType.MESH
F32 = jnp.float32
BF16 = jnp.bfloat16
FAR = (5, 4, 3, 7, 1, 2, 6)


def dot(a, b, contract):
    return lax.dot_general(a, b, (contract, ((), ())), preferred_element_type=F32)


NN = ((1,), (0,))
NT = ((1,), (1,))
TN = ((0,), (0,))


def split(value):
    high = value.astype(BF16)
    return high, (value - high.astype(F32)).astype(BF16)


def eye(rows, columns):
    return lax.broadcasted_iota(jnp.int32, (rows, columns), 0) == lax.broadcasted_iota(
        jnp.int32, (rows, columns), 1
    )


def write_rotation(x, w_ref):
    xh, xl = split(x)
    total = jnp.sum(jnp.sum(x * x, axis=0, keepdims=True), axis=1, keepdims=True)
    inv = 1.0 / jnp.sqrt(1.0 + total)
    b = 0.5 * inv * inv * inv
    a = 1.5 * inv - b
    left = dot(
        jnp.concatenate([xh, xl, xh], axis=1), jnp.concatenate([xh, xh, xl], axis=1), NT
    )
    right = dot(
        jnp.concatenate([xh, xl, xh], axis=0), jnp.concatenate([xh, xh, xl], axis=0), TN
    )
    lh, ll = split(left)
    cube = dot(
        jnp.concatenate([lh, ll, lh], axis=1), jnp.concatenate([xh, xh, xl], axis=0), NN
    )
    z = a * x - b * cube
    diagonal = jnp.where(eye(BW, BW), jnp.broadcast_to(a, (BW, BW)), 0.0)
    parts = (
        (0, 0, diagonal - b * left),
        (0, BW, z),
        (BW, 0, -z.T),
        (BW, BW, diagonal - b * right),
    )
    for row, column, value in parts:
        high, low = split(value)
        w_ref[row : row + BW, column : column + BW] = high
        w_ref[2 * BW + row : 3 * BW + row, column : column + BW] = low


def turn(hl, w_ref, column):
    wh = w_ref[0 : 2 * BW, column : column + BW]
    wl = w_ref[2 * BW : 4 * BW, column : column + BW]
    return dot(
        jnp.concatenate([hl, hl[:, : 2 * BW]], axis=1),
        jnp.concatenate([wh, wh, wl], axis=0),
        NN,
    )


def gram(ah, al, bh, bl):
    both = dot(ah, jnp.concatenate([bh, bl], axis=1), TN)
    return both[:, :BW] + both[:, BW:] + dot(al, bh, TN)


def pack(ts, slot, t, g, h):
    size = t.shape[0] // 4
    line = lax.broadcasted_iota(jnp.int32, (8, HB), 0)
    for j in range(8):
        half, quarter = j // 4, j % 4
        ts[slot, j, 0:size, :] = t[quarter * size : (quarter + 1) * size, half * HB : (half + 1) * HB]
        start = quarter * size
        wide = jnp.broadcast_to(g[:, start // HB * HB : start // HB * HB + HB], (8, HB))
        if start % HB:
            wide = pltpu.roll(wide, HB - start % HB, 1)
        lower = jnp.broadcast_to(h[:, half * HB : (half + 1) * HB], (8, HB))
        ts[slot, j, size : size + 8, :] = jnp.where(line == 0, wide, lower)


def jacobi(
    op, hl_out, x_out,
    pin, hl1, hl2, w, sb, ra, rl, raw, xn, hsum,
    ts0, ts1, ts2, tr0, tr1, tr2, rs0, rs1, rs2, rd0, rd1, rd2, xb0, xb1, xb2,
    load_sem, out_sem, core_send, core_recv, rs_send, rs_recv, ag_send, ag_recv,
    fw_send, fw_recv, z_send, z_recv, rl_send, rl_recv,
    raw_send, raw_recv, xz_send, xz_recv,
):
    blk = lax.axis_index("blk")
    rows = lax.axis_index("rows")
    blocks = lax.axis_size("blk")
    last = blocks - 1
    middle = blocks // 2
    is_relay = (blk == 0) | (blk == last)
    is_middle = (blk == middle - 1) | (blk == middle)
    late = is_relay | is_middle
    core = rows % 2
    chip = rows // 2
    px, py = rows // 4, chip % 2
    plain = pin.shape[2] - 256
    sizes, kinds = (320, 320, 128, 256), (0, 0, 1, 2)
    pieces = [(sum(sizes[:m]), sizes[m]) for m in range(len(sizes))]
    direct = sum(size for size, kind in zip(sizes, kinds) if kind == 0)
    count = len(sizes)
    tail = pl.ds(plain, 256)
    sibling = (blk, chip * 2 + 1 - core)
    other = 1 - core
    slots = (other, core)

    def mate(k):
        return ((px + k // 2) % 4) * 2 + (py + k % 2) % 2

    def source(k):
        return ((px + 4 - k // 2) % 4) * 2 + (py + k % 2) % 2

    def at_edge(slot):
        return blk == slot * last

    def crosses(slot):
        return blk == middle - slot

    def ahead(slot):
        return jnp.logical_not(at_edge(slot) | crosses(slot))

    def beside(slot):
        return (jnp.clip(blk + 2 * slot - 1, 0, last), rows)

    def columns(slot):
        shift = jnp.where((slot == 0) & (blk > 0), BW, 0)
        return slot * 2 * BW + shift, slot * 2 * BW + BW - shift

    loads = {}
    for i, slot in enumerate(slots):
        for part, column in enumerate(columns(slot)):
            loads[i, part] = pltpu.make_async_copy(
                op.at[:, pl.ds(pl.multiple_of(column, BW), BW)],
                pin.at[slot, part],
                load_sem.at[slot, part],
            )
            loads[i, part].start()

    barrier = pltpu.get_barrier_semaphore()
    pl.semaphore_signal(barrier, inc=1, device_id=sibling, device_id_type=MESH)
    for k in FAR:
        pl.semaphore_signal(
            barrier, inc=1, device_id=(blk, mate(k) * 2 + core), device_id_type=MESH
        )

    @pl.when(blk > 0)
    def _():
        pl.semaphore_signal(barrier, inc=1, device_id=(blk - 1, rows), device_id_type=MESH)

    @pl.when(blk < last)
    def _():
        pl.semaphore_signal(barrier, inc=1, device_id=(blk + 1, rows), device_id_type=MESH)

    @pl.when(is_relay)
    def _():
        for side in range(2):
            pl.semaphore_signal(
                barrier, inc=1, device_id=(middle - side, rows), device_id_type=MESH
            )

    @pl.when(is_middle)
    def _():
        for end in (0, last):
            pl.semaphore_signal(barrier, inc=1, device_id=(end, rows), device_id_type=MESH)

    greetings = 8 + jnp.where(blk > 0, 1, 0) + jnp.where(blk < last, 1, 0)
    greetings = greetings + jnp.where(is_relay | is_middle, 2, 0)
    pending = []

    def remote(src, dst, send, recv, target):
        return pltpu.make_async_remote_copy(
            src_ref=src, dst_ref=dst, send_sem=send, recv_sem=recv,
            device_id=target, device_id_type=MESH,
        )

    def core_copy(i, ts, tr):
        return remote(ts.at[other], tr, core_send.at[i], core_recv.at[i], sibling)

    def raw_copy(slot, part):
        return remote(
            op.at[pl.ds(plain, 256), pl.ds(pl.multiple_of(columns(slot)[part], BW), BW)],
            raw.at[1 - slot, part], raw_send.at[slot, part], raw_recv.at[1 - slot, part],
            beside(slot),
        )

    def raw_wait(slot, part):
        remote(
            raw.at[slot, part], raw.at[slot, part], raw_send.at[slot, part],
            raw_recv.at[slot, part], sibling,
        ).wait_recv()

    def x_away():
        return remote(xb0.at[core, chip], xn.at[other, chip], xz_send, xz_recv, beside(core))

    def x_spread(k):
        piece = xn.at[other, chip]
        if k == 0:
            return remote(piece, piece, fw_send.at[3, 0], fw_recv.at[3, 0], sibling)
        return remote(
            piece, piece, ag_send.at[3, k], ag_recv.at[3, k], (blk, mate(k) * 2 + core)
        )

    def x_hand(k):
        piece = xn.at[other, source(k)]
        return remote(piece, piece, fw_send.at[3, k], fw_recv.at[3, k], sibling)

    def rs_copy(i, k, rs, rd):
        return remote(
            rs.at[mate(k)], rd.at[k], rs_send.at[i, k], rs_recv.at[i, k],
            (blk, mate(k) * 2 + core),
        )

    def ag_copy(i, k, xb):
        piece = xb.at[core, chip]
        if k == 0:
            return remote(piece, piece, fw_send.at[i, 0], fw_recv.at[i, 0], sibling)
        return remote(
            piece, piece, ag_send.at[i, k], ag_recv.at[i, k], (blk, mate(k) * 2 + core)
        )

    def scatter(i, ts, tr, rs, rd):
        core_copy(i, ts, tr).wait_recv()
        for k in FAR:
            rs[mate(k)] = ts[core, mate(k)] + tr[mate(k)]
            rs_copy(i, k, rs, rd).start()

    def gather(i, ts, tr, rs, rd, xb, sign):
        size = rs.shape[1] - 8
        total = ts[core, chip] + tr[chip]
        for k in FAR[::-1]:
            rs_copy(i, k, rs, rd).wait_recv()
            total = total + rd[k]
        g = jnp.sum(
            jnp.where(eye(size, HB), jnp.broadcast_to(total[size : size + 1], (size, HB)), 0.0),
            axis=1, keepdims=True,
        )
        h = total[size + 1 : size + 2]
        xb[core, chip] = sign * total[:size] / (g + h + 1e-06)
        for k in FAR + (0,):
            ag_copy(i, k, xb).start()

    def hand_on(i, xb):
        for k in FAR[::-1]:
            piece = xb.at[core, source(k)]
            remote(
                piece, piece, ag_send.at[i, k], ag_recv.at[i, k], (blk, mate(k) * 2 + core)
            ).wait_recv()
            copy = remote(piece, piece, fw_send.at[i, k], fw_recv.at[i, k], sibling)
            copy.start()
            pending.append(copy)

    def receive_other(i, xb):
        for k in (0,) + FAR[::-1]:
            piece = xb.at[other, source(k)]
            remote(piece, piece, fw_send.at[i, k], fw_recv.at[i, k], sibling).wait_recv()

    for i, slot in enumerate(slots):
        loads[i, 0].wait()
        loads[i, 1].wait()

        def part(n, sums, slot=slot):
            at = pl.ds(pl.multiple_of(n * HB, HB), HB)
            out = []
            for p in range(2):
                value = pin[slot, p, at, :]
                high, low = split(value)
                hl1[slot, at, p * BW : (p + 1) * BW] = high
                hl1[slot, at, (2 + p) * BW : (3 + p) * BW] = low
                out.append(sums[p] + jnp.sum(value * value, axis=0, keepdims=True))
            return tuple(out)

        zero = jnp.zeros((1, BW), F32)
        g, h = lax.fori_loop(0, pin.shape[2] // HB, part, (zero, zero))
        t = gram(
            hl1[slot, :, 0:BW], hl1[slot, :, 2 * BW : 3 * BW],
            hl1[slot, :, BW : 2 * BW], hl1[slot, :, 3 * BW : 4 * BW],
        )
        pack(ts0, slot, t, g, h)
        if i == 0:
            pl.semaphore_wait(barrier, greetings)
            copy = core_copy(0, ts0, tr0)
            copy.start()
            pending.append(copy)
            for n in slots:

                @pl.when(ahead(n))
                def _(n=n):
                    for p in range(2):
                        raw_copy(n, p).start()

    sign = jnp.where((core == 0) & (blk > 0), 1.0, -1.0)
    scatter(0, ts0, tr0, rs0, rd0)
    gather(0, ts0, tr0, rs0, rd0, xb0, sign)

    @pl.when(ahead(core))
    def _():
        x_away().start()

    def spread():
        piece = xn.at[other, chip]
        remote(piece, piece, xz_send, xz_recv, sibling).wait_recv()
        for k in FAR + (0,):
            x_spread(k).start()

    pl.when(ahead(other) & (is_relay | is_middle))(spread)
    hand_on(0, xb0)

    def rows_of(m):
        return pl.ds(*pieces[m])


    def z_away(slot, column, m):
        at = rows_of(m)
        return remote(
            sb.at[slot, column, at], ra.at[1 - slot, column, at],
            z_send.at[slot, column, m], z_recv.at[1 - slot, column, m], beside(slot),
        )

    def z_here(slot, column, m):
        at = rows_of(m)
        return pltpu.make_async_copy(
            sb.at[slot, column, at], ra.at[slot, column, at], z_recv.at[slot, column, m]
        )

    def held(m):
        return pl.ds(pieces[m][0] - direct, pieces[m][1])

    def z_relay(slot, column, m):
        return remote(
            sb.at[slot, column, rows_of(m)], rl.at[column, held(m)],
            z_send.at[slot, column, m], rl_recv.at[column, m], (last * slot, rows),
        )

    def z_start(slot, column, m):
        @pl.when(at_edge(slot))
        def _():
            z_here(slot, column, m).start()

        if kinds[m] < 2:

            @pl.when(jnp.logical_not(at_edge(slot)) if kinds[m] == 0 else ahead(slot))
            def _():
                z_away(slot, column, m).start()

        if kinds[m] > 0:

            @pl.when(crosses(slot))
            def _():
                z_relay(slot, column, m).start()

    def relay(column, m):
        goal = jnp.where(blk == last, 0, 1)
        return remote(
            rl.at[column, held(m)], ra.at[goal, column, rows_of(m)],
            rl_send.at[column, m], z_recv.at[goal, column, m], (middle - goal, rows),
        )

    def pass_on(column):
        @pl.when(is_relay)
        def _():
            for m in (2, 3, 0, 1):
                if kinds[m] == 0:
                    continue
                piece = rl.at[column, held(m)]
                remote(
                    piece, piece, rl_send.at[column, m], rl_recv.at[column, m], sibling
                ).wait_recv()
                relay(column, m).start()

    def z_wait_recv(slot, column, m):
        at = rows_of(m)

        @pl.when(at_edge(slot))
        def _():
            z_here(slot, column, m).wait()

        @pl.when(jnp.logical_not(at_edge(slot)) if kinds[m] < 2 else crosses(slot))
        def _():
            remote(
                sb.at[slot, column, at], ra.at[slot, column, at],
                z_send.at[slot, column, m], z_recv.at[slot, column, m], sibling,
            ).wait_recv()

    def whole_x(xb, slot):
        return jnp.concatenate(
            [jnp.concatenate([xb[slot, 4 * p + n] for n in range(4)], axis=0) for p in range(2)],
            axis=1,
        )

    def move(slot, m):
        at = rows_of(m)
        moved = turn(hl1[slot, at, :], w.at[slot], 0)
        sb[slot, 0, at, :] = moved[:, :HB]
        z_start(slot, 0, m)
        sb[slot, 1, at, :] = moved[:, HB:]

    def order(do, slot):
        for m in (2, 3, 0, 1):
            if kinds[m] == 2:
                pl.when(jnp.logical_not(ahead(slot)))(functools.partial(do, m))
            else:
                do(m)

    for i, slot in enumerate((core, other)):
        if i == 1:

            pl.when(ahead(other) & jnp.logical_not(is_relay | is_middle))(spread)

            receive_other(0, xb0)
        write_rotation(whole_x(xb0, slot), w.at[slot])
        order(lambda m, slot=slot: move(slot, m), slot)
    for slot in (core, other):
        order(lambda m, slot=slot: z_start(slot, 1, m), slot)
    half_rows = pin.shape[2] // 2
    for slot in (core, other):
        h = jnp.zeros((1, BW), F32)
        for m in range(2):
            at = pl.ds(m * half_rows, half_rows)
            kept = turn(hl1[slot, at, :], w.at[slot], BW)
            high, low = split(kept)
            hl2[1 - slot, at, BW : 2 * BW] = high
            hl2[1 - slot, at, 3 * BW : 4 * BW] = low
            h = h + jnp.sum(kept * kept, axis=0, keepdims=True)
        hsum[1 - slot] = jnp.broadcast_to(h, (8, BW))

    pass_on(0)

    @pl.when(ahead(other))
    def _():
        for k in FAR[::-1]:
            piece = xn.at[other, source(k)]
            remote(
                piece, piece, ag_send.at[3, k], ag_recv.at[3, k], (blk, mate(k) * 2 + core)
            ).wait_recv()
            x_hand(k).start()

    for i, slot in enumerate((other, core)):

        @pl.when(ahead(slot))
        def _(i=i, slot=slot):
            if i == 1:
                for k in (0,) + FAR[::-1]:
                    piece = xn.at[core, source(k)]
                    remote(
                        piece, piece, fw_send.at[3, k], fw_recv.at[3, k], sibling
                    ).wait_recv()
            write_rotation(whole_x(xn, slot), w.at[slot])
            for p in range(2):
                raw_wait(slot, p)
            ah, al = split(raw[slot, 0])
            bh, bl = split(raw[slot, 1])
            turned = turn(jnp.concatenate([ah, bh, al, bl], axis=1), w.at[slot], 0)
            ra[slot, 0, tail, :] = turned[:, :HB]
            ra[slot, 1, tail, :] = turned[:, HB:]

    sign = jnp.where(core == 0, -1.0, 1.0)
    second = ((ts1, tr1, rs1, rd1, xb1), (ts2, tr2, rs2, rd2, xb2))
    for column, (ts, tr, rs, rd, xb) in enumerate(second):
        for i, slot in enumerate(slots):
            for m in range(count):
                z_wait_recv(slot, column, m)

            def part(n, g, slot=slot, column=column):
                at = pl.ds(pl.multiple_of(n * HB, HB), HB)
                value = ra[slot, column, at, :]
                high, low = split(value)
                hl2[slot, at, column * HB : (column + 1) * HB] = high
                hl2[slot, at, 2 * BW + column * HB : 2 * BW + (column + 1) * HB] = low
                return g + jnp.sum(value * value, axis=0, keepdims=True)

            g = lax.fori_loop(0, pin.shape[2] // HB, part, jnp.zeros((1, HB), F32))
            t = gram(
                hl2[slot, :, column * HB : (column + 1) * HB],
                hl2[slot, :, 2 * BW + column * HB : 2 * BW + (column + 1) * HB],
                hl2[slot, :, BW : 2 * BW], hl2[slot, :, 3 * BW : 4 * BW],
            )
            pack(ts, slot, t, g, hsum[slot, 0:1, :])
            if i == 0:
                copy = core_copy(1 + column, ts, tr)
                copy.start()
                pending.append(copy)
        if column == 0:
            scatter(1, ts, tr, rs, rd)
            pass_on(1)

            @pl.when(jnp.logical_not(late))
            def _():
                gather(1, *second[0], sign)

    whole = pltpu.make_async_copy(hl2, hl_out, out_sem.at[0])
    whole.start()

    @pl.when(late)
    def _():
        gather(1, *second[0], sign)

    scatter(2, *second[1][:4])
    hand_on(1, xb1)
    gather(2, *second[1], sign)
    hand_on(2, xb2)
    outs = []
    for column, xb in enumerate((xb1, xb2)):
        receive_other(1 + column, xb)
        copy = pltpu.make_async_copy(xb, x_out.at[column], out_sem.at[1 + column])
        copy.start()
        outs.append(copy)
    for copy in pending:
        copy.wait_send()
    for i, (rs, rd, xb) in enumerate(((rs0, rd0, xb0), (rs1, rd1, xb1), (rs2, rd2, xb2))):
        for k in FAR:
            rs_copy(i, k, rs, rd).wait_send()
        for k in FAR + (0,):
            ag_copy(i, k, xb).wait_send()
    for slot in range(2):

        @pl.when(jnp.logical_not(at_edge(slot)))
        def _(slot=slot):
            for column in range(2):
                for m in range(count):
                    if kinds[m] == 0:
                        z_away(slot, column, m).wait_send()

        @pl.when(crosses(slot))
        def _(slot=slot):
            for column in range(2):
                for m in range(count):
                    if kinds[m] > 0:
                        z_relay(slot, column, m).wait_send()

        @pl.when(ahead(slot))
        def _(slot=slot):
            for p in range(2):
                for m in range(count):
                    if kinds[m] == 1:
                        z_away(slot, p, m).wait_send()
                raw_copy(slot, p).wait_send()

    @pl.when(ahead(core))
    def _():
        x_away().wait_send()

    @pl.when(ahead(other))
    def _():
        for k in FAR + (0,):
            x_spread(k).wait_send()
        for k in FAR:
            x_hand(k).wait_send()

    @pl.when(is_relay)
    def _():
        for column in range(2):
            for m in range(count):
                if kinds[m] > 0:
                    relay(column, m).wait_send()

    whole.wait()
    for copy in outs:
        copy.wait()


def finish(hl_in, x_in, out, hl, xv, w, ob, hl_sem, x_sem, out_sem):
    count = 2
    size = hl.shape[1] // count
    x_copy = pltpu.make_async_copy(x_in, xv, x_sem)
    x_copy.start()
    loads = {}
    for slot in range(2):
        for m in range(count):
            at = pl.ds(m * size, size)
            loads[slot, m] = pltpu.make_async_copy(
                hl_in.at[slot, at], hl.at[slot, at], hl_sem.at[slot, m]
            )
            loads[slot, m].start()
    x_copy.wait()
    stores = []
    for slot in range(2):
        x = jnp.concatenate(
            [
                jnp.concatenate(
                    [xv[column, slot, 4 * p + n] for column in range(2) for n in range(4)], axis=0
                )
                for p in range(2)
            ],
            axis=1,
        )
        write_rotation(x, w.at[slot])
        for m in range(count):
            at = pl.ds(m * size, size)
            loads[slot, m].wait()
            lhs = hl[slot, at, :]
            first = slot * 2 * BW
            for p in range(2):
                column = first + (p * BW if slot == 0 else BW - p * BW)
                ob[at, column : column + BW] = turn(lhs, w.at[slot], p * BW)
            copy = pltpu.make_async_copy(
                ob.at[at, pl.ds(first, 2 * BW)],
                out.at[at, pl.ds(first, 2 * BW)],
                out_sem.at[slot, m],
            )
            copy.start()
            stores.append(copy)
    for copy in stores:
        copy.wait()


def local(operator):
    rows = operator.shape[0]
    any_spec = pl.BlockSpec(memory_space=pl.ANY)
    dma = pltpu.SemaphoreType.DMA

    def per_step(make):
        return [make(64), make(32), make(32)]

    hl, x = pl.pallas_call(
        jacobi,
        out_shape=(
            jax.ShapeDtypeStruct((2, rows, 4 * BW), BF16),
            jax.ShapeDtypeStruct((2, 2, 8, 32, HB), F32),
        ),
        in_specs=[any_spec],
        out_specs=(any_spec, any_spec),
        scratch_shapes=[
            pltpu.VMEM((2, 2, rows, BW), F32),
            pltpu.VMEM((2, rows, 4 * BW), BF16),
            pltpu.VMEM((2, rows, 4 * BW), BF16),
            pltpu.VMEM((2, 4 * BW, 2 * BW), BF16),
            pltpu.VMEM((2, 2, rows, HB), F32),
            pltpu.VMEM((2, 2, rows, HB), F32),
            pltpu.VMEM((2, rows - sum(s for s, k in zip((320, 320, 128, 256), (0, 0, 1, 2)) if k == 0), HB), F32),
            pltpu.VMEM((2, 2, 256, BW), F32),
            pltpu.VMEM((2, 8, 64, HB), F32),
            pltpu.VMEM((2, 8, BW), F32),
            *per_step(lambda size: pltpu.VMEM((2, 8, size + 8, HB), F32)),
            *per_step(lambda size: pltpu.VMEM((8, size + 8, HB), F32)),
            *per_step(lambda size: pltpu.VMEM((8, size + 8, HB), F32)),
            *per_step(lambda size: pltpu.VMEM((8, size + 8, HB), F32)),
            *per_step(lambda size: pltpu.VMEM((2, 8, size, HB), F32)),
            dma((2, 2)),
            dma((3,)),
            dma((3,)),
            dma((3,)),
            dma((3, 8)),
            dma((3, 8)),
            dma((4, 8)),
            dma((4, 8)),
            dma((4, 8)),
            dma((4, 8)),
            dma((2, 2, 8)),
            dma((2, 2, 8)),
            dma((2, 8)),
            dma((2, 8)),
            dma((2, 2)),
            dma((2, 2)),
            dma,
            dma,
        ],
        compiler_params=pltpu.CompilerParams(
            collective_id=0, has_side_effects=True, vmem_limit_bytes=48 * 2**20
        ),
        name="jacobi",
    )(operator)
    return pl.pallas_call(
        finish,
        out_shape=jax.ShapeDtypeStruct(operator.shape, F32),
        in_specs=[any_spec, any_spec],
        out_specs=any_spec,
        scratch_shapes=[
            pltpu.VMEM((2, rows, 4 * BW), BF16),
            pltpu.VMEM((2, 2, 8, 32, HB), F32),
            pltpu.VMEM((2, 4 * BW, 2 * BW), BF16),
            pltpu.VMEM((rows, 4 * BW), F32),
            dma((2, 2)),
            dma,
            dma((2, 2)),
        ],
        compiler_params=pltpu.CompilerParams(vmem_limit_bytes=40 * 2**20),
        name="finish",
    )(hl, x)


def solution(mesh):
    placed = P("rows", "blk")
    return jax.shard_map(local, mesh=mesh, in_specs=(placed,), out_specs=placed, check_vma=False)
```

```python
import functools

import jax
import jax.numpy as jnp
from jax import lax
from jax.experimental import pallas as pl
from jax.experimental.pallas import tpu as pltpu
from jax.sharding import PartitionSpec as P

BW = 256
HB = 128
MESH = pl.DeviceIdType.MESH
F32 = jnp.float32
BF16 = jnp.bfloat16
FAR = (5, 4, 3, 7, 1, 2, 6)


def dot(a, b, contract):
    return lax.dot_general(a, b, (contract, ((), ())), preferred_element_type=F32)


NN = ((1,), (0,))
NT = ((1,), (1,))
TN = ((0,), (0,))


def split(value):
    high = value.astype(BF16)
    return high, (value - high.astype(F32)).astype(BF16)


def eye(rows, columns):
    return lax.broadcasted_iota(jnp.int32, (rows, columns), 0) == lax.broadcasted_iota(
        jnp.int32, (rows, columns), 1
    )


def write_rotation(x, w_ref):
    xh, xl = split(x)
    total = jnp.sum(jnp.sum(x * x, axis=0, keepdims=True), axis=1, keepdims=True)
    inv = 1.0 / jnp.sqrt(1.0 + total)
    b = 0.5 * inv * inv * inv
    a = 1.5 * inv - b
    left = dot(
        jnp.concatenate([xh, xl, xh], axis=1), jnp.concatenate([xh, xh, xl], axis=1), NT
    )
    right = dot(
        jnp.concatenate([xh, xl, xh], axis=0), jnp.concatenate([xh, xh, xl], axis=0), TN
    )
    lh, ll = split(left)
    cube = dot(
        jnp.concatenate([lh, ll, lh], axis=1), jnp.concatenate([xh, xh, xl], axis=0), NN
    )
    z = a * x - b * cube
    diagonal = jnp.where(eye(BW, BW), jnp.broadcast_to(a, (BW, BW)), 0.0)
    parts = (
        (0, 0, diagonal - b * left),
        (0, BW, z),
        (BW, 0, -z.T),
        (BW, BW, diagonal - b * right),
    )
    for row, column, value in parts:
        high, low = split(value)
        w_ref[row : row + BW, column : column + BW] = high
        w_ref[2 * BW + row : 3 * BW + row, column : column + BW] = low


def turn(hl, w_ref, column):
    wh = w_ref[0 : 2 * BW, column : column + BW]
    wl = w_ref[2 * BW : 4 * BW, column : column + BW]
    return dot(
        jnp.concatenate([hl, hl[:, : 2 * BW]], axis=1),
        jnp.concatenate([wh, wh, wl], axis=0),
        NN,
    )


def gram(ah, al, bh, bl):
    both = dot(ah, jnp.concatenate([bh, bl], axis=1), TN)
    return both[:, :BW] + both[:, BW:] + dot(al, bh, TN)


def pack(ts, slot, t, g, h):
    size = t.shape[0] // 4
    line = lax.broadcasted_iota(jnp.int32, (8, HB), 0)
    for j in range(8):
        half, quarter = j // 4, j % 4
        ts[slot, j, 0:size, :] = t[quarter * size : (quarter + 1) * size, half * HB : (half + 1) * HB]
        start = quarter * size
        wide = jnp.broadcast_to(g[:, start // HB * HB : start // HB * HB + HB], (8, HB))
        if start % HB:
            wide = pltpu.roll(wide, HB - start % HB, 1)
        lower = jnp.broadcast_to(h[:, half * HB : (half + 1) * HB], (8, HB))
        ts[slot, j, size : size + 8, :] = jnp.where(line == 0, wide, lower)


def jacobi(
    op, hl_out, x_out,
    pin, hl1, hl2, w, sb, ra, rl, raw, xn, hsum,
    ts0, ts1, ts2, tr0, tr1, tr2, rs0, rs1, rs2, rd0, rd1, rd2, xb0, xb1, xb2,
    load_sem, out_sem, core_send, core_recv, rs_send, rs_recv, ag_send, ag_recv,
    fw_send, fw_recv, z_send, z_recv, rl_send, rl_recv,
    raw_send, raw_recv, xz_send, xz_recv,
):
    blk = lax.axis_index("blk")
    rows = lax.axis_index("rows")
    blocks = lax.axis_size("blk")
    last = blocks - 1
    middle = blocks // 2
    is_relay = (blk == 0) | (blk == last)
    is_middle = (blk == middle - 1) | (blk == middle)
    late = is_relay | is_middle
    core = rows % 2
    chip = rows // 2
    px, py = rows // 4, chip % 2
    plain = pin.shape[2] - 256
    sizes, kinds = (320, 320, 128, 256), (0, 0, 1, 2)
    pieces = [(sum(sizes[:m]), sizes[m]) for m in range(len(sizes))]
    direct = sum(size for size, kind in zip(sizes, kinds) if kind == 0)
    count = len(sizes)
    tail = pl.ds(plain, 256)
    sibling = (blk, chip * 2 + 1 - core)
    other = 1 - core
    slots = (other, core)

    def mate(k):
        return ((px + k // 2) % 4) * 2 + (py + k % 2) % 2

    def source(k):
        return ((px + 4 - k // 2) % 4) * 2 + (py + k % 2) % 2

    def at_edge(slot):
        return blk == slot * last

    def crosses(slot):
        return blk == middle - slot

    def ahead(slot):
        return jnp.logical_not(at_edge(slot) | crosses(slot))

    def beside(slot):
        return (jnp.clip(blk + 2 * slot - 1, 0, last), rows)

    def columns(slot):
        shift = jnp.where((slot == 0) & (blk > 0), BW, 0)
        return slot * 2 * BW + shift, slot * 2 * BW + BW - shift

    loads = {}
    for i, slot in enumerate(slots):
        for part, column in enumerate(columns(slot)):
            loads[i, part] = pltpu.make_async_copy(
                op.at[:, pl.ds(pl.multiple_of(column, BW), BW)],
                pin.at[slot, part],
                load_sem.at[slot, part],
            )
            loads[i, part].start()

    barrier = pltpu.get_barrier_semaphore()
    pl.semaphore_signal(barrier, inc=1, device_id=sibling, device_id_type=MESH)
    for k in FAR:
        pl.semaphore_signal(
            barrier, inc=1, device_id=(blk, mate(k) * 2 + core), device_id_type=MESH
        )

    @pl.when(blk > 0)
    def _():
        pl.semaphore_signal(barrier, inc=1, device_id=(blk - 1, rows), device_id_type=MESH)

    @pl.when(blk < last)
    def _():
        pl.semaphore_signal(barrier, inc=1, device_id=(blk + 1, rows), device_id_type=MESH)

    @pl.when(is_relay)
    def _():
        for side in range(2):
            pl.semaphore_signal(
                barrier, inc=1, device_id=(middle - side, rows), device_id_type=MESH
            )

    @pl.when(is_middle)
    def _():
        for end in (0, last):
            pl.semaphore_signal(barrier, inc=1, device_id=(end, rows), device_id_type=MESH)

    greetings = 8 + jnp.where(blk > 0, 1, 0) + jnp.where(blk < last, 1, 0)
    greetings = greetings + jnp.where(is_relay | is_middle, 2, 0)
    pending = []

    def remote(src, dst, send, recv, target):
        return pltpu.make_async_remote_copy(
            src_ref=src, dst_ref=dst, send_sem=send, recv_sem=recv,
            device_id=target, device_id_type=MESH,
        )

    def core_copy(i, ts, tr):
        return remote(ts.at[other], tr, core_send.at[i], core_recv.at[i], sibling)

    def raw_copy(slot, part):
        return remote(
            op.at[pl.ds(plain, 256), pl.ds(pl.multiple_of(columns(slot)[part], BW), BW)],
            raw.at[1 - slot, part], raw_send.at[slot, part], raw_recv.at[1 - slot, part],
            beside(slot),
        )

    def raw_wait(slot, part):
        remote(
            raw.at[slot, part], raw.at[slot, part], raw_send.at[slot, part],
            raw_recv.at[slot, part], sibling,
        ).wait_recv()

    def x_away():
        return remote(xb0.at[core, chip], xn.at[other, chip], xz_send, xz_recv, beside(core))

    def x_spread(k):
        piece = xn.at[other, chip]
        if k == 0:
            return remote(piece, piece, fw_send.at[3, 0], fw_recv.at[3, 0], sibling)
        return remote(
            piece, piece, ag_send.at[3, k], ag_recv.at[3, k], (blk, mate(k) * 2 + core)
        )

    def x_hand(k):
        piece = xn.at[other, source(k)]
        return remote(piece, piece, fw_send.at[3, k], fw_recv.at[3, k], sibling)

    def rs_copy(i, k, rs, rd):
        return remote(
            rs.at[mate(k)], rd.at[k], rs_send.at[i, k], rs_recv.at[i, k],
            (blk, mate(k) * 2 + core),
        )

    def ag_copy(i, k, xb):
        piece = xb.at[core, chip]
        if k == 0:
            return remote(piece, piece, fw_send.at[i, 0], fw_recv.at[i, 0], sibling)
        return remote(
            piece, piece, ag_send.at[i, k], ag_recv.at[i, k], (blk, mate(k) * 2 + core)
        )

    def scatter(i, ts, tr, rs, rd):
        core_copy(i, ts, tr).wait_recv()
        for k in FAR:
            rs[mate(k)] = ts[core, mate(k)] + tr[mate(k)]
            rs_copy(i, k, rs, rd).start()

    def gather(i, ts, tr, rs, rd, xb, sign):
        size = rs.shape[1] - 8
        total = ts[core, chip] + tr[chip]
        for k in FAR[::-1]:
            rs_copy(i, k, rs, rd).wait_recv()
            total = total + rd[k]
        g = jnp.sum(
            jnp.where(eye(size, HB), jnp.broadcast_to(total[size : size + 1], (size, HB)), 0.0),
            axis=1, keepdims=True,
        )
        h = total[size + 1 : size + 2]
        xb[core, chip] = sign * total[:size] / (g + h + 1e-06)
        for k in FAR + (0,):
            ag_copy(i, k, xb).start()

    def hand_on(i, xb):
        for k in FAR[::-1]:
            piece = xb.at[core, source(k)]
            remote(
                piece, piece, ag_send.at[i, k], ag_recv.at[i, k], (blk, mate(k) * 2 + core)
            ).wait_recv()
            copy = remote(piece, piece, fw_send.at[i, k], fw_recv.at[i, k], sibling)
            copy.start()
            pending.append(copy)

    def receive_other(i, xb):
        for k in (0,) + FAR[::-1]:
            piece = xb.at[other, source(k)]
            remote(piece, piece, fw_send.at[i, k], fw_recv.at[i, k], sibling).wait_recv()

    for i, slot in enumerate(slots):
        loads[i, 0].wait()
        loads[i, 1].wait()

        def part(n, sums, slot=slot):
            at = pl.ds(pl.multiple_of(n * HB, HB), HB)
            out = []
            for p in range(2):
                value = pin[slot, p, at, :]
                high, low = split(value)
                hl1[slot, at, p * BW : (p + 1) * BW] = high
                hl1[slot, at, (2 + p) * BW : (3 + p) * BW] = low
                out.append(sums[p] + jnp.sum(value * value, axis=0, keepdims=True))
            return tuple(out)

        zero = jnp.zeros((1, BW), F32)
        g, h = lax.fori_loop(0, pin.shape[2] // HB, part, (zero, zero))
        t = gram(
            hl1[slot, :, 0:BW], hl1[slot, :, 2 * BW : 3 * BW],
            hl1[slot, :, BW : 2 * BW], hl1[slot, :, 3 * BW : 4 * BW],
        )
        pack(ts0, slot, t, g, h)
        if i == 0:
            pl.semaphore_wait(barrier, greetings)
            copy = core_copy(0, ts0, tr0)
            copy.start()
            pending.append(copy)
            for n in slots:

                @pl.when(ahead(n))
                def _(n=n):
                    for p in range(2):
                        raw_copy(n, p).start()

    sign = jnp.where((core == 0) & (blk > 0), 1.0, -1.0)
    scatter(0, ts0, tr0, rs0, rd0)
    gather(0, ts0, tr0, rs0, rd0, xb0, sign)

    @pl.when(ahead(core))
    def _():
        x_away().start()

    def spread():
        piece = xn.at[other, chip]
        remote(piece, piece, xz_send, xz_recv, sibling).wait_recv()
        for k in FAR + (0,):
            x_spread(k).start()

    pl.when(ahead(other) & (is_relay | is_middle))(spread)
    hand_on(0, xb0)

    def rows_of(m):
        return pl.ds(*pieces[m])


    def z_away(slot, column, m):
        at = rows_of(m)
        return remote(
            sb.at[slot, column, at], ra.at[1 - slot, column, at],
            z_send.at[slot, column, m], z_recv.at[1 - slot, column, m], beside(slot),
        )

    def z_here(slot, column, m):
        at = rows_of(m)
        return pltpu.make_async_copy(
            sb.at[slot, column, at], ra.at[slot, column, at], z_recv.at[slot, column, m]
        )

    def held(m):
        return pl.ds(pieces[m][0] - direct, pieces[m][1])

    def z_relay(slot, column, m):
        return remote(
            sb.at[slot, column, rows_of(m)], rl.at[column, held(m)],
            z_send.at[slot, column, m], rl_recv.at[column, m], (last * slot, rows),
        )

    def z_start(slot, column, m):
        @pl.when(at_edge(slot))
        def _():
            z_here(slot, column, m).start()

        if kinds[m] < 2:

            @pl.when(jnp.logical_not(at_edge(slot)) if kinds[m] == 0 else ahead(slot))
            def _():
                z_away(slot, column, m).start()

        if kinds[m] > 0:

            @pl.when(crosses(slot))
            def _():
                z_relay(slot, column, m).start()

    def relay(column, m):
        goal = jnp.where(blk == last, 0, 1)
        return remote(
            rl.at[column, held(m)], ra.at[goal, column, rows_of(m)],
            rl_send.at[column, m], z_recv.at[goal, column, m], (middle - goal, rows),
        )

    def pass_on(column):
        @pl.when(is_relay)
        def _():
            for m in (2, 3, 0, 1):
                if kinds[m] == 0:
                    continue
                piece = rl.at[column, held(m)]
                remote(
                    piece, piece, rl_send.at[column, m], rl_recv.at[column, m], sibling
                ).wait_recv()
                relay(column, m).start()

    def z_wait_recv(slot, column, m):
        at = rows_of(m)

        @pl.when(at_edge(slot))
        def _():
            z_here(slot, column, m).wait()

        @pl.when(jnp.logical_not(at_edge(slot)) if kinds[m] < 2 else crosses(slot))
        def _():
            remote(
                sb.at[slot, column, at], ra.at[slot, column, at],
                z_send.at[slot, column, m], z_recv.at[slot, column, m], sibling,
            ).wait_recv()

    def whole_x(xb, slot):
        return jnp.concatenate(
            [jnp.concatenate([xb[slot, 4 * p + n] for n in range(4)], axis=0) for p in range(2)],
            axis=1,
        )

    def move(slot, m):
        at = rows_of(m)
        moved = turn(hl1[slot, at, :], w.at[slot], 0)
        sb[slot, 0, at, :] = moved[:, :HB]
        z_start(slot, 0, m)
        sb[slot, 1, at, :] = moved[:, HB:]

    def order(do, slot):
        for m in (2, 3, 0, 1):
            if kinds[m] == 2:
                pl.when(jnp.logical_not(ahead(slot)))(functools.partial(do, m))
            else:
                do(m)

    for i, slot in enumerate((core, other)):
        if i == 1:

            pl.when(ahead(other) & jnp.logical_not(is_relay | is_middle))(spread)

            receive_other(0, xb0)
        write_rotation(whole_x(xb0, slot), w.at[slot])
        order(lambda m, slot=slot: move(slot, m), slot)
    for slot in (core, other):
        order(lambda m, slot=slot: z_start(slot, 1, m), slot)
    half_rows = pin.shape[2] // 2
    for slot in (core, other):
        h = jnp.zeros((1, BW), F32)
        for m in range(2):
            at = pl.ds(m * half_rows, half_rows)
            kept = turn(hl1[slot, at, :], w.at[slot], BW)
            high, low = split(kept)
            hl2[1 - slot, at, BW : 2 * BW] = high
            hl2[1 - slot, at, 3 * BW : 4 * BW] = low
            h = h + jnp.sum(kept * kept, axis=0, keepdims=True)
        hsum[1 - slot] = jnp.broadcast_to(h, (8, BW))

    pass_on(0)

    @pl.when(ahead(other))
    def _():
        for k in FAR[::-1]:
            piece = xn.at[other, source(k)]
            remote(
                piece, piece, ag_send.at[3, k], ag_recv.at[3, k], (blk, mate(k) * 2 + core)
            ).wait_recv()
            x_hand(k).start()

    for i, slot in enumerate((other, core)):

        @pl.when(ahead(slot))
        def _(i=i, slot=slot):
            if i == 1:
                for k in (0,) + FAR[::-1]:
                    piece = xn.at[core, source(k)]
                    remote(
                        piece, piece, fw_send.at[3, k], fw_recv.at[3, k], sibling
                    ).wait_recv()
            write_rotation(whole_x(xn, slot), w.at[slot])
            for p in range(2):
                raw_wait(slot, p)
            ah, al = split(raw[slot, 0])
            bh, bl = split(raw[slot, 1])
            turned = turn(jnp.concatenate([ah, bh, al, bl], axis=1), w.at[slot], 0)
            ra[slot, 0, tail, :] = turned[:, :HB]
            ra[slot, 1, tail, :] = turned[:, HB:]

    sign = jnp.where(core == 0, -1.0, 1.0)
    second = ((ts1, tr1, rs1, rd1, xb1), (ts2, tr2, rs2, rd2, xb2))
    for column, (ts, tr, rs, rd, xb) in enumerate(second):
        for i, slot in enumerate(slots):
            for m in range(count):
                z_wait_recv(slot, column, m)

            def part(n, g, slot=slot, column=column):
                at = pl.ds(pl.multiple_of(n * HB, HB), HB)
                value = ra[slot, column, at, :]
                high, low = split(value)
                hl2[slot, at, column * HB : (column + 1) * HB] = high
                hl2[slot, at, 2 * BW + column * HB : 2 * BW + (column + 1) * HB] = low
                return g + jnp.sum(value * value, axis=0, keepdims=True)

            g = lax.fori_loop(0, pin.shape[2] // HB, part, jnp.zeros((1, HB), F32))
            t = gram(
                hl2[slot, :, column * HB : (column + 1) * HB],
                hl2[slot, :, 2 * BW + column * HB : 2 * BW + (column + 1) * HB],
                hl2[slot, :, BW : 2 * BW], hl2[slot, :, 3 * BW : 4 * BW],
            )
            pack(ts, slot, t, g, hsum[slot, 0:1, :])
            if i == 0:
                copy = core_copy(1 + column, ts, tr)
                copy.start()
                pending.append(copy)
        if column == 0:
            scatter(1, ts, tr, rs, rd)
            pass_on(1)

            @pl.when(jnp.logical_not(late))
            def _():
                gather(1, *second[0], sign)

    whole = pltpu.make_async_copy(hl2, hl_out, out_sem.at[0])
    whole.start()

    @pl.when(late)
    def _():
        gather(1, *second[0], sign)

    scatter(2, *second[1][:4])
    hand_on(1, xb1)
    gather(2, *second[1], sign)
    hand_on(2, xb2)
    outs = []
    for column, xb in enumerate((xb1, xb2)):
        receive_other(1 + column, xb)
        copy = pltpu.make_async_copy(xb, x_out.at[column], out_sem.at[1 + column])
        copy.start()
        outs.append(copy)
    for copy in pending:
        copy.wait_send()
    for i, (rs, rd, xb) in enumerate(((rs0, rd0, xb0), (rs1, rd1, xb1), (rs2, rd2, xb2))):
        for k in FAR:
            rs_copy(i, k, rs, rd).wait_send()
        for k in FAR + (0,):
            ag_copy(i, k, xb).wait_send()
    for slot in range(2):

        @pl.when(jnp.logical_not(at_edge(slot)))
        def _(slot=slot):
            for column in range(2):
                for m in range(count):
                    if kinds[m] == 0:
                        z_away(slot, column, m).wait_send()

        @pl.when(crosses(slot))
        def _(slot=slot):
            for column in range(2):
                for m in range(count):
                    if kinds[m] > 0:
                        z_relay(slot, column, m).wait_send()

        @pl.when(ahead(slot))
        def _(slot=slot):
            for p in range(2):
                for m in range(count):
                    if kinds[m] == 1:
                        z_away(slot, p, m).wait_send()
                raw_copy(slot, p).wait_send()

    @pl.when(ahead(core))
    def _():
        x_away().wait_send()

    @pl.when(ahead(other))
    def _():
        for k in FAR + (0,):
            x_spread(k).wait_send()
        for k in FAR:
            x_hand(k).wait_send()

    @pl.when(is_relay)
    def _():
        for column in range(2):
            for m in range(count):
                if kinds[m] > 0:
                    relay(column, m).wait_send()

    whole.wait()
    for copy in outs:
        copy.wait()


def finish(hl_in, x_in, out, hl, xv, w, ob, hl_sem, x_sem, out_sem):
    count = 2
    size = hl.shape[1] // count
    x_copy = pltpu.make_async_copy(x_in, xv, x_sem)
    x_copy.start()
    loads = {}
    for slot in range(2):
        for m in range(count):
            at = pl.ds(m * size, size)
            loads[slot, m] = pltpu.make_async_copy(
                hl_in.at[slot, at], hl.at[slot, at], hl_sem.at[slot, m]
            )
            loads[slot, m].start()
    x_copy.wait()
    for load in loads.values():
        load.wait()
    for slot in range(2):
        x = jnp.concatenate(
            [
                jnp.concatenate(
                    [xv[column, slot, 4 * p + n] for column in range(2) for n in range(4)], axis=0
                )
                for p in range(2)
            ],
            axis=1,
        )
        write_rotation(x, w.at[slot])
    stores = []
    for slot in range(2):
        for m in range(count):
            at = pl.ds(m * size, size)
            lhs = hl[slot, at, :]
            first = slot * 2 * BW
            for p in range(2):
                column = first + (p * BW if slot == 0 else BW - p * BW)
                ob[at, column : column + BW] = turn(lhs, w.at[slot], p * BW)
            copy = pltpu.make_async_copy(
                ob.at[at, pl.ds(first, 2 * BW)],
                out.at[at, pl.ds(first, 2 * BW)],
                out_sem.at[slot, m],
            )
            copy.start()
            stores.append(copy)
    for copy in stores:
        copy.wait()


def local(operator):
    rows = operator.shape[0]
    any_spec = pl.BlockSpec(memory_space=pl.ANY)
    dma = pltpu.SemaphoreType.DMA

    def per_step(make):
        return [make(64), make(32), make(32)]

    hl, x = pl.pallas_call(
        jacobi,
        out_shape=(
            jax.ShapeDtypeStruct((2, rows, 4 * BW), BF16),
            jax.ShapeDtypeStruct((2, 2, 8, 32, HB), F32),
        ),
        in_specs=[any_spec],
        out_specs=(any_spec, any_spec),
        scratch_shapes=[
            pltpu.VMEM((2, 2, rows, BW), F32),
            pltpu.VMEM((2, rows, 4 * BW), BF16),
            pltpu.VMEM((2, rows, 4 * BW), BF16),
            pltpu.VMEM((2, 4 * BW, 2 * BW), BF16),
            pltpu.VMEM((2, 2, rows, HB), F32),
            pltpu.VMEM((2, 2, rows, HB), F32),
            pltpu.VMEM((2, rows - sum(s for s, k in zip((320, 320, 128, 256), (0, 0, 1, 2)) if k == 0), HB), F32),
            pltpu.VMEM((2, 2, 256, BW), F32),
            pltpu.VMEM((2, 8, 64, HB), F32),
            pltpu.VMEM((2, 8, BW), F32),
            *per_step(lambda size: pltpu.VMEM((2, 8, size + 8, HB), F32)),
            *per_step(lambda size: pltpu.VMEM((8, size + 8, HB), F32)),
            *per_step(lambda size: pltpu.VMEM((8, size + 8, HB), F32)),
            *per_step(lambda size: pltpu.VMEM((8, size + 8, HB), F32)),
            *per_step(lambda size: pltpu.VMEM((2, 8, size, HB), F32)),
            dma((2, 2)),
            dma((3,)),
            dma((3,)),
            dma((3,)),
            dma((3, 8)),
            dma((3, 8)),
            dma((4, 8)),
            dma((4, 8)),
            dma((4, 8)),
            dma((4, 8)),
            dma((2, 2, 8)),
            dma((2, 2, 8)),
            dma((2, 8)),
            dma((2, 8)),
            dma((2, 2)),
            dma((2, 2)),
            dma,
            dma,
        ],
        compiler_params=pltpu.CompilerParams(
            collective_id=0, has_side_effects=True, vmem_limit_bytes=48 * 2**20
        ),
        name="jacobi",
    )(operator)
    return pl.pallas_call(
        finish,
        out_shape=jax.ShapeDtypeStruct(operator.shape, F32),
        in_specs=[any_spec, any_spec],
        out_specs=any_spec,
        scratch_shapes=[
            pltpu.VMEM((2, rows, 4 * BW), BF16),
            pltpu.VMEM((2, 2, 8, 32, HB), F32),
            pltpu.VMEM((2, 4 * BW, 2 * BW), BF16),
            pltpu.VMEM((rows, 4 * BW), F32),
            dma((2, 2)),
            dma,
            dma((2, 2)),
        ],
        compiler_params=pltpu.CompilerParams(vmem_limit_bytes=40 * 2**20),
        name="finish",
    )(hl, x)


def solution(mesh):
    placed = P("rows", "blk")
    return jax.shard_map(local, mesh=mesh, in_specs=(placed,), out_specs=placed, check_vma=False)
```

```python
import functools

import jax
import jax.numpy as jnp
from jax import lax
from jax.experimental import pallas as pl
from jax.experimental.pallas import tpu as pltpu
from jax.sharding import PartitionSpec as P

BW = 256
HB = 128
MESH = pl.DeviceIdType.MESH
F32 = jnp.float32
BF16 = jnp.bfloat16
FAR = (5, 4, 3, 7, 1, 2, 6)


def dot(a, b, contract):
    return lax.dot_general(a, b, (contract, ((), ())), preferred_element_type=F32)


NN = ((1,), (0,))
NT = ((1,), (1,))
TN = ((0,), (0,))


def split(value):
    high = value.astype(BF16)
    return high, (value - high.astype(F32)).astype(BF16)


def eye(rows, columns):
    return lax.broadcasted_iota(jnp.int32, (rows, columns), 0) == lax.broadcasted_iota(
        jnp.int32, (rows, columns), 1
    )


def write_rotation(x, w_ref):
    xh, xl = split(x)
    total = jnp.sum(jnp.sum(x * x, axis=0, keepdims=True), axis=1, keepdims=True)
    inv = 1.0 / jnp.sqrt(1.0 + total)
    b = 0.5 * inv * inv * inv
    a = 1.5 * inv - b
    left = dot(
        jnp.concatenate([xh, xl, xh], axis=1), jnp.concatenate([xh, xh, xl], axis=1), NT
    )
    right = dot(
        jnp.concatenate([xh, xl, xh], axis=0), jnp.concatenate([xh, xh, xl], axis=0), TN
    )
    lh, ll = split(left)
    cube = dot(
        jnp.concatenate([lh, ll, lh], axis=1), jnp.concatenate([xh, xh, xl], axis=0), NN
    )
    z = a * x - b * cube
    diagonal = jnp.where(eye(BW, BW), jnp.broadcast_to(a, (BW, BW)), 0.0)
    parts = (
        (0, 0, diagonal - b * left),
        (0, BW, z),
        (BW, 0, -z.T),
        (BW, BW, diagonal - b * right),
    )
    for row, column, value in parts:
        high, low = split(value)
        w_ref[row : row + BW, column : column + BW] = high
        w_ref[2 * BW + row : 3 * BW + row, column : column + BW] = low


def turn(hl, w_ref, column):
    wh = w_ref[0 : 2 * BW, column : column + BW]
    wl = w_ref[2 * BW : 4 * BW, column : column + BW]
    return dot(
        jnp.concatenate([hl, hl[:, : 2 * BW]], axis=1),
        jnp.concatenate([wh, wh, wl], axis=0),
        NN,
    )


def gram(ah, al, bh, bl):
    both = dot(ah, jnp.concatenate([bh, bl], axis=1), TN)
    return both[:, :BW] + both[:, BW:] + dot(al, bh, TN)


def pack(ts, slot, t, g, h):
    size = t.shape[0] // 4
    line = lax.broadcasted_iota(jnp.int32, (8, HB), 0)
    for j in range(8):
        half, quarter = j // 4, j % 4
        ts[slot, j, 0:size, :] = t[quarter * size : (quarter + 1) * size, half * HB : (half + 1) * HB]
        start = quarter * size
        wide = jnp.broadcast_to(g[:, start // HB * HB : start // HB * HB + HB], (8, HB))
        if start % HB:
            wide = pltpu.roll(wide, HB - start % HB, 1)
        lower = jnp.broadcast_to(h[:, half * HB : (half + 1) * HB], (8, HB))
        ts[slot, j, size : size + 8, :] = jnp.where(line == 0, wide, lower)


def jacobi(
    op, hl_out, x_out,
    pin, hl1, hl2, w, sb, ra, rl, raw, xn, hsum,
    ts0, ts1, ts2, tr0, tr1, tr2, rs0, rs1, rs2, rd0, rd1, rd2, xb0, xb1, xb2,
    load_sem, out_sem, core_send, core_recv, rs_send, rs_recv, ag_send, ag_recv,
    fw_send, fw_recv, z_send, z_recv, rl_send, rl_recv,
    raw_send, raw_recv, xz_send, xz_recv,
):
    blk = lax.axis_index("blk")
    rows = lax.axis_index("rows")
    blocks = lax.axis_size("blk")
    last = blocks - 1
    middle = blocks // 2
    is_relay = (blk == 0) | (blk == last)
    is_middle = (blk == middle - 1) | (blk == middle)
    late = is_relay | is_middle
    core = rows % 2
    chip = rows // 2
    px, py = rows // 4, chip % 2
    plain = pin.shape[2] - 256
    sizes, kinds = (320, 320, 128, 256), (0, 0, 1, 2)
    pieces = [(sum(sizes[:m]), sizes[m]) for m in range(len(sizes))]
    direct = sum(size for size, kind in zip(sizes, kinds) if kind == 0)
    count = len(sizes)
    tail = pl.ds(plain, 256)
    sibling = (blk, chip * 2 + 1 - core)
    other = 1 - core
    slots = (other, core)

    def mate(k):
        return ((px + k // 2) % 4) * 2 + (py + k % 2) % 2

    def source(k):
        return ((px + 4 - k // 2) % 4) * 2 + (py + k % 2) % 2

    def at_edge(slot):
        return blk == slot * last

    def crosses(slot):
        return blk == middle - slot

    def ahead(slot):
        return jnp.logical_not(at_edge(slot) | crosses(slot))

    def beside(slot):
        return (jnp.clip(blk + 2 * slot - 1, 0, last), rows)

    def columns(slot):
        shift = jnp.where((slot == 0) & (blk > 0), BW, 0)
        return slot * 2 * BW + shift, slot * 2 * BW + BW - shift

    loads = {}
    for i, slot in enumerate(slots):
        for part, column in enumerate(columns(slot)):
            loads[i, part] = pltpu.make_async_copy(
                op.at[:, pl.ds(pl.multiple_of(column, BW), BW)],
                pin.at[slot, part],
                load_sem.at[slot, part],
            )
            loads[i, part].start()

    barrier = pltpu.get_barrier_semaphore()
    pl.semaphore_signal(barrier, inc=1, device_id=sibling, device_id_type=MESH)
    for k in FAR:
        pl.semaphore_signal(
            barrier, inc=1, device_id=(blk, mate(k) * 2 + core), device_id_type=MESH
        )

    @pl.when(blk > 0)
    def _():
        pl.semaphore_signal(barrier, inc=1, device_id=(blk - 1, rows), device_id_type=MESH)

    @pl.when(blk < last)
    def _():
        pl.semaphore_signal(barrier, inc=1, device_id=(blk + 1, rows), device_id_type=MESH)

    @pl.when(is_relay)
    def _():
        for side in range(2):
            pl.semaphore_signal(
                barrier, inc=1, device_id=(middle - side, rows), device_id_type=MESH
            )

    @pl.when(is_middle)
    def _():
        for end in (0, last):
            pl.semaphore_signal(barrier, inc=1, device_id=(end, rows), device_id_type=MESH)

    greetings = 8 + jnp.where(blk > 0, 1, 0) + jnp.where(blk < last, 1, 0)
    greetings = greetings + jnp.where(is_relay | is_middle, 2, 0)
    pending = []

    def remote(src, dst, send, recv, target):
        return pltpu.make_async_remote_copy(
            src_ref=src, dst_ref=dst, send_sem=send, recv_sem=recv,
            device_id=target, device_id_type=MESH,
        )

    def core_copy(i, ts, tr):
        return remote(ts.at[other], tr, core_send.at[i], core_recv.at[i], sibling)

    def raw_copy(slot, part):
        return remote(
            op.at[pl.ds(plain, 256), pl.ds(pl.multiple_of(columns(slot)[part], BW), BW)],
            raw.at[1 - slot, part], raw_send.at[slot, part], raw_recv.at[1 - slot, part],
            beside(slot),
        )

    def raw_wait(slot, part):
        remote(
            raw.at[slot, part], raw.at[slot, part], raw_send.at[slot, part],
            raw_recv.at[slot, part], sibling,
        ).wait_recv()

    def x_away():
        return remote(xb0.at[core, chip], xn.at[other, chip], xz_send, xz_recv, beside(core))

    def x_spread(k):
        piece = xn.at[other, chip]
        if k == 0:
            return remote(piece, piece, fw_send.at[3, 0], fw_recv.at[3, 0], sibling)
        return remote(
            piece, piece, ag_send.at[3, k], ag_recv.at[3, k], (blk, mate(k) * 2 + core)
        )

    def x_hand(k):
        piece = xn.at[other, source(k)]
        return remote(piece, piece, fw_send.at[3, k], fw_recv.at[3, k], sibling)

    def rs_copy(i, k, rs, rd):
        return remote(
            rs.at[mate(k)], rd.at[k], rs_send.at[i, k], rs_recv.at[i, k],
            (blk, mate(k) * 2 + core),
        )

    def ag_copy(i, k, xb):
        piece = xb.at[core, chip]
        if k == 0:
            return remote(piece, piece, fw_send.at[i, 0], fw_recv.at[i, 0], sibling)
        return remote(
            piece, piece, ag_send.at[i, k], ag_recv.at[i, k], (blk, mate(k) * 2 + core)
        )

    def scatter(i, ts, tr, rs, rd):
        core_copy(i, ts, tr).wait_recv()
        for k in FAR:
            rs[mate(k)] = ts[core, mate(k)] + tr[mate(k)]
            rs_copy(i, k, rs, rd).start()

    def gather(i, ts, tr, rs, rd, xb, sign):
        size = rs.shape[1] - 8
        total = ts[core, chip] + tr[chip]
        for k in FAR[::-1]:
            rs_copy(i, k, rs, rd).wait_recv()
            total = total + rd[k]
        g = jnp.sum(
            jnp.where(eye(size, HB), jnp.broadcast_to(total[size : size + 1], (size, HB)), 0.0),
            axis=1, keepdims=True,
        )
        h = total[size + 1 : size + 2]
        xb[core, chip] = sign * total[:size] / (g + h + 1e-06)
        for k in FAR + (0,):
            ag_copy(i, k, xb).start()

    def hand_on(i, xb):
        for k in FAR[::-1]:
            piece = xb.at[core, source(k)]
            remote(
                piece, piece, ag_send.at[i, k], ag_recv.at[i, k], (blk, mate(k) * 2 + core)
            ).wait_recv()
            copy = remote(piece, piece, fw_send.at[i, k], fw_recv.at[i, k], sibling)
            copy.start()
            pending.append(copy)

    def receive_other(i, xb):
        for k in (0,) + FAR[::-1]:
            piece = xb.at[other, source(k)]
            remote(piece, piece, fw_send.at[i, k], fw_recv.at[i, k], sibling).wait_recv()

    for i, slot in enumerate(slots):
        loads[i, 0].wait()
        loads[i, 1].wait()

        def part(n, sums, slot=slot):
            at = pl.ds(pl.multiple_of(n * HB, HB), HB)
            out = []
            for p in range(2):
                value = pin[slot, p, at, :]
                high, low = split(value)
                hl1[slot, at, p * BW : (p + 1) * BW] = high
                hl1[slot, at, (2 + p) * BW : (3 + p) * BW] = low
                out.append(sums[p] + jnp.sum(value * value, axis=0, keepdims=True))
            return tuple(out)

        zero = jnp.zeros((1, BW), F32)
        g, h = lax.fori_loop(0, pin.shape[2] // HB, part, (zero, zero))
        t = gram(
            hl1[slot, :, 0:BW], hl1[slot, :, 2 * BW : 3 * BW],
            hl1[slot, :, BW : 2 * BW], hl1[slot, :, 3 * BW : 4 * BW],
        )
        pack(ts0, slot, t, g, h)
        if i == 0:
            pl.semaphore_wait(barrier, greetings)
            copy = core_copy(0, ts0, tr0)
            copy.start()
            pending.append(copy)
            for n in slots:

                @pl.when(ahead(n))
                def _(n=n):
                    for p in range(2):
                        raw_copy(n, p).start()

    sign = jnp.where((core == 0) & (blk > 0), 1.0, -1.0)
    scatter(0, ts0, tr0, rs0, rd0)
    gather(0, ts0, tr0, rs0, rd0, xb0, sign)

    @pl.when(ahead(core))
    def _():
        x_away().start()

    def spread():
        piece = xn.at[other, chip]
        remote(piece, piece, xz_send, xz_recv, sibling).wait_recv()
        for k in FAR + (0,):
            x_spread(k).start()

    pl.when(ahead(other) & (is_relay | is_middle))(spread)
    hand_on(0, xb0)

    def rows_of(m):
        return pl.ds(*pieces[m])


    def z_away(slot, column, m):
        at = rows_of(m)
        return remote(
            sb.at[slot, column, at], ra.at[1 - slot, column, at],
            z_send.at[slot, column, m], z_recv.at[1 - slot, column, m], beside(slot),
        )

    def z_here(slot, column, m):
        at = rows_of(m)
        return pltpu.make_async_copy(
            sb.at[slot, column, at], ra.at[slot, column, at], z_recv.at[slot, column, m]
        )

    def held(m):
        return pl.ds(pieces[m][0] - direct, pieces[m][1])

    def z_relay(slot, column, m):
        return remote(
            sb.at[slot, column, rows_of(m)], rl.at[column, held(m)],
            z_send.at[slot, column, m], rl_recv.at[column, m], (last * slot, rows),
        )

    def z_start(slot, column, m):
        @pl.when(at_edge(slot))
        def _():
            z_here(slot, column, m).start()

        if kinds[m] < 2:

            @pl.when(jnp.logical_not(at_edge(slot)) if kinds[m] == 0 else ahead(slot))
            def _():
                z_away(slot, column, m).start()

        if kinds[m] > 0:

            @pl.when(crosses(slot))
            def _():
                z_relay(slot, column, m).start()

    def relay(column, m):
        goal = jnp.where(blk == last, 0, 1)
        return remote(
            rl.at[column, held(m)], ra.at[goal, column, rows_of(m)],
            rl_send.at[column, m], z_recv.at[goal, column, m], (middle - goal, rows),
        )

    def pass_on(column):
        @pl.when(is_relay)
        def _():
            for m in (2, 3, 0, 1):
                if kinds[m] == 0:
                    continue
                piece = rl.at[column, held(m)]
                remote(
                    piece, piece, rl_send.at[column, m], rl_recv.at[column, m], sibling
                ).wait_recv()
                relay(column, m).start()

    def z_wait_recv(slot, column, m):
        at = rows_of(m)

        @pl.when(at_edge(slot))
        def _():
            z_here(slot, column, m).wait()

        @pl.when(jnp.logical_not(at_edge(slot)) if kinds[m] < 2 else crosses(slot))
        def _():
            remote(
                sb.at[slot, column, at], ra.at[slot, column, at],
                z_send.at[slot, column, m], z_recv.at[slot, column, m], sibling,
            ).wait_recv()

    def whole_x(xb, slot):
        return jnp.concatenate(
            [jnp.concatenate([xb[slot, 4 * p + n] for n in range(4)], axis=0) for p in range(2)],
            axis=1,
        )

    def move(slot, m):
        at = rows_of(m)
        moved = turn(hl1[slot, at, :], w.at[slot], 0)
        sb[slot, 0, at, :] = moved[:, :HB]
        z_start(slot, 0, m)
        sb[slot, 1, at, :] = moved[:, HB:]

    def order(do, slot):
        for m in (2, 3, 0, 1):
            if kinds[m] == 2:
                pl.when(jnp.logical_not(ahead(slot)))(functools.partial(do, m))
            else:
                do(m)

    for i, slot in enumerate((core, other)):
        if i == 1:

            pl.when(ahead(other) & jnp.logical_not(is_relay | is_middle))(spread)

            receive_other(0, xb0)
        write_rotation(whole_x(xb0, slot), w.at[slot])
        order(lambda m, slot=slot: move(slot, m), slot)
    for slot in (core, other):
        order(lambda m, slot=slot: z_start(slot, 1, m), slot)
    half_rows = pin.shape[2] // 2
    for slot in (core, other):
        h = jnp.zeros((1, BW), F32)
        for m in range(2):
            at = pl.ds(m * half_rows, half_rows)
            kept = turn(hl1[slot, at, :], w.at[slot], BW)
            high, low = split(kept)
            hl2[1 - slot, at, BW : 2 * BW] = high
            hl2[1 - slot, at, 3 * BW : 4 * BW] = low
            h = h + jnp.sum(kept * kept, axis=0, keepdims=True)
        hsum[1 - slot] = jnp.broadcast_to(h, (8, BW))

    pass_on(0)

    @pl.when(ahead(other))
    def _():
        for k in FAR[::-1]:
            piece = xn.at[other, source(k)]
            remote(
                piece, piece, ag_send.at[3, k], ag_recv.at[3, k], (blk, mate(k) * 2 + core)
            ).wait_recv()
            x_hand(k).start()

    for i, slot in enumerate((other, core)):

        @pl.when(ahead(slot))
        def _(i=i, slot=slot):
            if i == 1:
                for k in (0,) + FAR[::-1]:
                    piece = xn.at[core, source(k)]
                    remote(
                        piece, piece, fw_send.at[3, k], fw_recv.at[3, k], sibling
                    ).wait_recv()
            write_rotation(whole_x(xn, slot), w.at[slot])
            for p in range(2):
                raw_wait(slot, p)
            ah, al = split(raw[slot, 0])
            bh, bl = split(raw[slot, 1])
            turned = turn(jnp.concatenate([ah, bh, al, bl], axis=1), w.at[slot], 0)
            ra[slot, 0, tail, :] = turned[:, :HB]
            ra[slot, 1, tail, :] = turned[:, HB:]

    sign = jnp.where(core == 0, -1.0, 1.0)
    second = ((ts1, tr1, rs1, rd1, xb1), (ts2, tr2, rs2, rd2, xb2))
    for column, (ts, tr, rs, rd, xb) in enumerate(second):
        for i, slot in enumerate(slots):
            for m in range(count):
                z_wait_recv(slot, column, m)

            def part(n, g, slot=slot, column=column):
                at = pl.ds(pl.multiple_of(n * HB, HB), HB)
                value = ra[slot, column, at, :]
                high, low = split(value)
                hl2[slot, at, column * HB : (column + 1) * HB] = high
                hl2[slot, at, 2 * BW + column * HB : 2 * BW + (column + 1) * HB] = low
                return g + jnp.sum(value * value, axis=0, keepdims=True)

            g = lax.fori_loop(0, pin.shape[2] // HB, part, jnp.zeros((1, HB), F32))
            t = gram(
                hl2[slot, :, column * HB : (column + 1) * HB],
                hl2[slot, :, 2 * BW + column * HB : 2 * BW + (column + 1) * HB],
                hl2[slot, :, BW : 2 * BW], hl2[slot, :, 3 * BW : 4 * BW],
            )
            pack(ts, slot, t, g, hsum[slot, 0:1, :])
            if i == 0:
                copy = core_copy(1 + column, ts, tr)
                copy.start()
                pending.append(copy)
        if column == 0:
            scatter(1, ts, tr, rs, rd)
            pass_on(1)

            @pl.when(jnp.logical_not(late))
            def _():
                gather(1, *second[0], sign)

    whole = pltpu.make_async_copy(hl2, hl_out, out_sem.at[0])
    whole.start()

    @pl.when(late)
    def _():
        gather(1, *second[0], sign)

    scatter(2, *second[1][:4])
    hand_on(1, xb1)
    gather(2, *second[1], sign)
    receive_other(1, xb1)
    outs = [pltpu.make_async_copy(xb1, x_out.at[0], out_sem.at[1])]
    outs[0].start()

    for copy in pending:
        copy.wait_send()
    pending.clear()
    for i, (rs, rd, xb) in enumerate(((rs0, rd0, xb0), (rs1, rd1, xb1), (rs2, rd2, xb2))):
        for k in FAR:
            rs_copy(i, k, rs, rd).wait_send()
        if i < 2:
            for k in FAR + (0,):
                ag_copy(i, k, xb).wait_send()
    for slot in range(2):

        @pl.when(jnp.logical_not(at_edge(slot)))
        def _(slot=slot):
            for column in range(2):
                for m in range(count):
                    if kinds[m] == 0:
                        z_away(slot, column, m).wait_send()

        @pl.when(crosses(slot))
        def _(slot=slot):
            for column in range(2):
                for m in range(count):
                    if kinds[m] > 0:
                        z_relay(slot, column, m).wait_send()

        @pl.when(ahead(slot))
        def _(slot=slot):
            for p in range(2):
                for m in range(count):
                    if kinds[m] == 1:
                        z_away(slot, p, m).wait_send()
                raw_copy(slot, p).wait_send()

    @pl.when(ahead(core))
    def _():
        x_away().wait_send()

    @pl.when(ahead(other))
    def _():
        for k in FAR + (0,):
            x_spread(k).wait_send()
        for k in FAR:
            x_hand(k).wait_send()

    @pl.when(is_relay)
    def _():
        for column in range(2):
            for m in range(count):
                if kinds[m] > 0:
                    relay(column, m).wait_send()

    whole.wait()
    hand_on(2, xb2)
    receive_other(2, xb2)
    outs.append(pltpu.make_async_copy(xb2, x_out.at[1], out_sem.at[2]))
    outs[1].start()
    for copy in pending:
        copy.wait_send()
    for k in FAR + (0,):
        ag_copy(2, k, xb2).wait_send()
    for copy in outs:
        copy.wait()


def finish(hl_in, x_in, out, hl, xv, w, ob, hl_sem, x_sem, out_sem):
    count = 2
    size = hl.shape[1] // count
    x_copy = pltpu.make_async_copy(x_in, xv, x_sem)
    x_copy.start()
    loads = {}
    for slot in range(2):
        for m in range(count):
            at = pl.ds(m * size, size)
            loads[slot, m] = pltpu.make_async_copy(
                hl_in.at[slot, at], hl.at[slot, at], hl_sem.at[slot, m]
            )
            loads[slot, m].start()
    x_copy.wait()
    for load in loads.values():
        load.wait()
    for slot in range(2):
        x = jnp.concatenate(
            [
                jnp.concatenate(
                    [xv[column, slot, 4 * p + n] for column in range(2) for n in range(4)], axis=0
                )
                for p in range(2)
            ],
            axis=1,
        )
        write_rotation(x, w.at[slot])
    stores = []
    for slot in range(2):
        for m in range(count):
            at = pl.ds(m * size, size)
            lhs = hl[slot, at, :]
            first = slot * 2 * BW
            for p in range(2):
                column = first + (p * BW if slot == 0 else BW - p * BW)
                ob[at, column : column + BW] = turn(lhs, w.at[slot], p * BW)
            copy = pltpu.make_async_copy(
                ob.at[at, pl.ds(first, 2 * BW)],
                out.at[at, pl.ds(first, 2 * BW)],
                out_sem.at[slot, m],
            )
            copy.start()
            stores.append(copy)
    for copy in stores:
        copy.wait()


def local(operator):
    rows = operator.shape[0]
    any_spec = pl.BlockSpec(memory_space=pl.ANY)
    dma = pltpu.SemaphoreType.DMA

    def per_step(make):
        return [make(64), make(32), make(32)]

    hl, x = pl.pallas_call(
        jacobi,
        out_shape=(
            jax.ShapeDtypeStruct((2, rows, 4 * BW), BF16),
            jax.ShapeDtypeStruct((2, 2, 8, 32, HB), F32),
        ),
        in_specs=[any_spec],
        out_specs=(any_spec, any_spec),
        scratch_shapes=[
            pltpu.VMEM((2, 2, rows, BW), F32),
            pltpu.VMEM((2, rows, 4 * BW), BF16),
            pltpu.VMEM((2, rows, 4 * BW), BF16),
            pltpu.VMEM((2, 4 * BW, 2 * BW), BF16),
            pltpu.VMEM((2, 2, rows, HB), F32),
            pltpu.VMEM((2, 2, rows, HB), F32),
            pltpu.VMEM((2, rows - sum(s for s, k in zip((320, 320, 128, 256), (0, 0, 1, 2)) if k == 0), HB), F32),
            pltpu.VMEM((2, 2, 256, BW), F32),
            pltpu.VMEM((2, 8, 64, HB), F32),
            pltpu.VMEM((2, 8, BW), F32),
            *per_step(lambda size: pltpu.VMEM((2, 8, size + 8, HB), F32)),
            *per_step(lambda size: pltpu.VMEM((8, size + 8, HB), F32)),
            *per_step(lambda size: pltpu.VMEM((8, size + 8, HB), F32)),
            *per_step(lambda size: pltpu.VMEM((8, size + 8, HB), F32)),
            *per_step(lambda size: pltpu.VMEM((2, 8, size, HB), F32)),
            dma((2, 2)),
            dma((3,)),
            dma((3,)),
            dma((3,)),
            dma((3, 8)),
            dma((3, 8)),
            dma((4, 8)),
            dma((4, 8)),
            dma((4, 8)),
            dma((4, 8)),
            dma((2, 2, 8)),
            dma((2, 2, 8)),
            dma((2, 8)),
            dma((2, 8)),
            dma((2, 2)),
            dma((2, 2)),
            dma,
            dma,
        ],
        compiler_params=pltpu.CompilerParams(
            collective_id=0, has_side_effects=True, vmem_limit_bytes=48 * 2**20
        ),
        name="jacobi",
    )(operator)
    return pl.pallas_call(
        finish,
        out_shape=jax.ShapeDtypeStruct(operator.shape, F32),
        in_specs=[any_spec, any_spec],
        out_specs=any_spec,
        scratch_shapes=[
            pltpu.VMEM((2, rows, 4 * BW), BF16),
            pltpu.VMEM((2, 2, 8, 32, HB), F32),
            pltpu.VMEM((2, 4 * BW, 2 * BW), BF16),
            pltpu.VMEM((rows, 4 * BW), F32),
            dma((2, 2)),
            dma,
            dma((2, 2)),
        ],
        compiler_params=pltpu.CompilerParams(vmem_limit_bytes=40 * 2**20),
        name="finish",
    )(hl, x)


def solution(mesh):
    placed = P("rows", "blk")
    return jax.shard_map(local, mesh=mesh, in_specs=(placed,), out_specs=placed, check_vma=False)
```
